32 devices in a mesh: dp: 2 (over y), tensor: 16 (over z, x, core).
Axes of the slice: x: 2, y: 2, z: 4, core: 2. Of those that a mesh axis runs over, the one named last changes fastest.
Arguments:
- hidden_in: bfloat16 [2, 16, 1, 64, 1536], P('dp', 'tensor'), may hold values from -6 to 6
- rotated_queries: bfloat16 [2, 16, 1, 64, 1536], P('dp', 'tensor'), may hold values from -8 to 8
- fresh_key_values: bfloat16 [2, 16, 1, 64, 1024], P('dp', 'tensor'), may hold values from -6 to 6
- cached_key_values: bfloat16 [2, 512, 1024], P('dp', 'tensor'), may hold values from -8 to 8
- cached_len: int32 [2], P('dp'), may hold values from 8 to 512, as said below
- expert_ids: int32 [2, 16, 1, 64, 8], P('dp', 'tensor'), may hold values from 0 to 15, all different within a row; in each aligned block of 64 rows (0 to 63, 64 to 127, ..., all dimensions but the last counted through in order) at most 33 rows name the same one
- route_gates: float32 [2, 16, 1, 64, 8], P('dp', 'tensor'), may hold values from 0.1 to 0.4
- output_weight: bfloat16 [1536, 1536], P('tensor'), may hold values from -3 to 3
- norm_gain: float32 [1536], replicated, may hold values from 0.1 to 1.9
- gate_up: bfloat16 [16, 1536, 1024], P('tensor', 'dp'), may hold values from -0.15625 to 0.15625
- down_weight: bfloat16 [16, 512, 1536], P('tensor', 'dp'), may hold values from -0.25 to 0.25
Outputs:
- hidden_out: bfloat16 [2, 16, 1, 64, 1536], P('dp', 'tensor')
- cache_out: bfloat16 [2, 1536, 1024], P('dp', None, 'tensor')
The draws below stay inside these ranges and needn't reach their ends.
Inputs may be any that keep to these rules, and one draw needn't show every extreme that they name: `cached_len`: some request has exactly 512 valid slots. `expert_ids`: among the 64 tokens of one device no expert is chosen more than 33 times, and on some device some expert is chosen exactly 33 times.
All inputs are finite; a program needn't handle non-finite values.
Results may differ from the reference program's by a relative error of at most 0.006.
Values may be sent and summed in bfloat16 or wider, within the bound.
A program may use at most 64 MiB of HBM per device.

```python
import math
import jax
import jax.numpy as jnp
import numpy as np
from jax import lax

MODEL_WIDTH = 1536
QUERY_HEADS = 24
KEY_VALUE_HEADS = 8
HEAD_WIDTH = 64
FFE = 512
TOPK = 8
REQ_GRP = 1
NEW_DEV = 64
REQUEST_COUNT = 2
FRESH_POSITIONS = 1024
CACHE_SLOT_LIMIT = 512
TOK_DEV = 64
KVW = 1024
EXPERTS = 16
CAP = 33
N_DP = 2
N_TENSOR = 16


def draw_rotated_queries(key, part):
    rows_all = N_DP * N_TENSOR * REQ_GRP * NEW_DEV
    sampled_values = jnp.clip(jax.random.normal(jax.random.fold_in(key, 11), (rows_all, QUERY_HEADS, HEAD_WIDTH), jnp.float32), -8.0, 8.0)
    return sampled_values.reshape(N_DP, N_TENSOR, REQ_GRP, NEW_DEV, QUERY_HEADS * HEAD_WIDTH).astype(jnp.bfloat16)


def draw_cached_key_values(key, part):
    complete_shape = (REQUEST_COUNT, CACHE_SLOT_LIMIT, KEY_VALUE_HEADS, 2 * HEAD_WIDTH)
    sampled_values = jnp.clip(jax.random.normal(jax.random.fold_in(key, 12), complete_shape, jnp.float32), -8.0, 8.0)
    return sampled_values.reshape(REQUEST_COUNT, CACHE_SLOT_LIMIT, 2 * KEY_VALUE_HEADS * HEAD_WIDTH).astype(jnp.bfloat16)


def draw_cached_len(key, part):
    lengths = jax.random.randint(jax.random.fold_in(key, 21), (REQUEST_COUNT,), 8, CACHE_SLOT_LIMIT + 1)
    picked = jax.random.randint(jax.random.fold_in(key, 22), (), 0, REQUEST_COUNT)
    return jnp.where(jnp.arange(REQUEST_COUNT) == picked, CACHE_SLOT_LIMIT, lengths).astype(jnp.int32)


def block_levels(key, shape, split, least, largest):
    gain = 1.0
    for position, parts in split:
        draws = jax.random.uniform(jax.random.fold_in(jax.random.fold_in(key, 6), position), (parts,), jnp.float32, least / len(split), largest / len(split))
        gain = gain * jnp.repeat(jnp.exp(draws), shape[position] // parts).reshape((-1,) + (1,) * (len(shape) - 1 - position))
    return gain


def deal_out(own_key, own, number, rows, number_of, top, limit, lean):
    order = jax.random.permutation(own_key, number_of)
    crowded, common = load_shares(number_of, rows * top, limit, lean, True), load_shares(number_of, rows * top, limit, lean, False)
    places = jnp.arange(number_of)

    def named(sizes, turn):
        used = int((sizes > 0).sum())
        fixed = max(1, used // 4)
        shifted = fixed + (places - fixed + turn * (used - fixed)) % max(1, number_of - fixed)
        return jnp.zeros((number_of,), jnp.int32).at[order[jnp.where(places < fixed, places, shifted)]].set(jnp.asarray(sizes, jnp.int32))

    sizes = jnp.where(number % 4 == 0, named(crowded, number // 4), named(common, number - number // 4 - 1))
    mixed = jax.random.permutation(jax.random.fold_in(own, 3), number_of)
    source_of, taker = mixed[0:number_of // 2 * 2:2], mixed[1:number_of // 2 * 2:2]
    margin = jnp.minimum(sizes[source_of] - 1, limit - sizes[taker]) // 2
    margin = jnp.where((source_of == order[0]) | (taker == order[0]) | (sizes[taker] == 0), 0, jnp.maximum(margin, 0))
    shifted = jax.random.randint(jax.random.fold_in(own, 4), (number_of // 2,), 0, 1 << 20) % (margin + 1)
    sizes = sizes.at[source_of].add(-shifted).at[taker].add(shifted)
    members = jnp.searchsorted(jnp.cumsum(sizes), jnp.arange(rows * top), side="right").astype(jnp.int32)
    grid = members.reshape(top, rows).T
    grid = grid[jax.random.permutation(jax.random.fold_in(own, 1), rows)]
    turn = jax.random.randint(jax.random.fold_in(own, 2), (rows, 1), 0, top)
    return jnp.take_along_axis(grid, (jnp.arange(top)[None, :] + turn) % top, axis=1)


def load_shares(amount, total, bound, lean, full):
    portions = [(1 << 20) // math.isqrt(standing ** lean) + 1 for standing in range(1, amount + 1)]
    largest = bound if full else min(bound, max(-(-total // amount), total * portions[0] // sum(portions)))
    least = 1 if total - largest >= amount - 1 else 0
    given, rest = [largest] + [least] * (amount - 1), total - largest - least * (amount - 1)
    while rest > 0:
        free = [i for i in range(1, amount) if given[i] < largest] or [i for i in range(1, amount) if given[i] < bound]
        whole, left = sum([portions[i] for i in free]), rest
        for i in free:
            addition = min(bound - given[i], max(1, left * portions[i] // whole), rest)
            given[i] = given[i] + addition
            rest = rest - addition
    return np.array(given)


def noise(stream_key, dims, width, most, pieces=(), held_as=jnp.bfloat16):
    drawn = jax.random.normal(stream_key, dims, jnp.float32) * width
    if len(pieces) > 0:
        drawn = block_levels(stream_key, dims, pieces, -0.22, 0.18) * drawn
    return jnp.clip(drawn, min=-most, max=most).astype(held_as)


def setup_inputs(seed: int = 0) -> dict:
    keys = jax.random.split(jax.random.key(seed), 12)
    hidden_in = noise(keys[0], (N_DP, N_TENSOR, REQ_GRP, NEW_DEV, MODEL_WIDTH), 1.0, 6.0, ((0, 2), (1, 16)))
    rotated_queries = draw_rotated_queries(jax.random.fold_in(keys[11], 71), 0)
    fresh_key_values = noise(keys[2], (N_DP, N_TENSOR, REQ_GRP, NEW_DEV, KVW), 1.0, 6.0, ((0, 2), (1, 16)))
    cached_key_values = draw_cached_key_values(jax.random.fold_in(keys[11], 71), 0)
    cached_len = draw_cached_len(jax.random.fold_in(keys[11], 71), 0)
    expert_ids_keys = jax.random.split(jax.random.fold_in(keys[5], 1), N_DP * N_TENSOR * REQ_GRP * NEW_DEV // TOK_DEV)
    expert_ids_turns = jax.random.permutation(jax.random.fold_in(keys[5], 3), N_DP * N_TENSOR * REQ_GRP * NEW_DEV // TOK_DEV)
    expert_ids = jax.vmap(lambda own, number: deal_out(jax.random.fold_in(keys[5], 2), own, number, TOK_DEV, EXPERTS, TOPK, CAP, 0))(expert_ids_keys, expert_ids_turns).reshape((N_DP, N_TENSOR, REQ_GRP, NEW_DEV, TOPK))
    route_gates = jnp.clip(0.1 + 0.3 * jax.random.uniform(keys[6], (N_DP, N_TENSOR, REQ_GRP, NEW_DEV, TOPK), jnp.float32) ** block_levels(keys[6], (N_DP, N_TENSOR, REQ_GRP, NEW_DEV, TOPK), ((0, 2), (1, 16)), -0.2, 0.2), 0.1, 0.4)
    output_weight = noise(keys[7], (QUERY_HEADS * HEAD_WIDTH, MODEL_WIDTH), 0.5, 3.0, ((0, 16),))
    norm_gain = jnp.clip(1.0 + 0.18 * jax.random.normal(keys[8], (MODEL_WIDTH,), jnp.float32), 0.1, 1.9)
    gate_up = noise(keys[9], (EXPERTS, MODEL_WIDTH, 2 * FFE), MODEL_WIDTH ** -0.5, 0.15625, ((0, 16), (1, 2)))
    down_weight = noise(keys[10], (EXPERTS, FFE, MODEL_WIDTH), FFE ** -0.5, 0.25, ((0, 16), (1, 2)))
    return {"hidden_in": hidden_in, "rotated_queries": rotated_queries, "fresh_key_values": fresh_key_values, "cached_key_values": cached_key_values, "cached_len": cached_len, "expert_ids": expert_ids, "route_gates": route_gates, "output_weight": output_weight, "norm_gain": norm_gain, "gate_up": gate_up, "down_weight": down_weight}


epsilon = 1e-05

def by_request(blocked):
    last_width = blocked.shape[-1]
    return jnp.transpose(blocked, (0, 2, 1, 3, 4)).reshape(N_DP * REQ_GRP, N_TENSOR * NEW_DEV, last_width)

def request_attention(single_query, single_fresh, single_cache, length, output_weight):
    query_groups = QUERY_HEADS // KEY_VALUE_HEADS
    query_matrix = jnp.transpose(single_query.reshape(FRESH_POSITIONS, KEY_VALUE_HEADS, query_groups, HEAD_WIDTH), (1, 0, 2, 3))
    key_value_part = jnp.concatenate([single_cache.reshape(CACHE_SLOT_LIMIT, KEY_VALUE_HEADS, 2 * HEAD_WIDTH), single_fresh.reshape(FRESH_POSITIONS, KEY_VALUE_HEADS, 2 * HEAD_WIDTH)], 0)
    key_value_part = jnp.transpose(key_value_part, (1, 0, 2))
    key_pos = jnp.arange(CACHE_SLOT_LIMIT + FRESH_POSITIONS, dtype=jnp.int32)
    query_pos = jnp.arange(FRESH_POSITIONS, dtype=jnp.int32)
    visible = jnp.where(key_pos[None, :] < CACHE_SLOT_LIMIT, key_pos[None, :] < length, key_pos[None, :] - CACHE_SLOT_LIMIT <= query_pos[:, None])
    visible = visible[:, None, :]

    def one_head(packed):
        query_head, pair_head = packed
        keys_all = pair_head[:, :HEAD_WIDTH].astype(jnp.float32)
        values_all = pair_head[:, HEAD_WIDTH:].astype(jnp.float32)
        scores = jnp.einsum('pgd,kd->pgk', query_head.astype(jnp.float32), keys_all) * (1.0 / math.sqrt(HEAD_WIDTH))
        scores = jnp.where(visible, scores, -1e+30)
        highest = lax.optimization_barrier(jnp.max(scores, -1, keepdims=True))
        weights = jnp.where(visible, jnp.exp(scores - highest), 0.0)
        denoms = lax.optimization_barrier(jnp.sum(weights, -1, keepdims=True))
        rounded = lax.optimization_barrier(weights.astype(jnp.bfloat16)).astype(jnp.float32)
        return jnp.einsum('pgk,kd->pgd', rounded, values_all) / denoms
    mixed_output = lax.map(one_head, (query_matrix, key_value_part))
    attention_result = jnp.transpose(mixed_output, (1, 0, 2, 3)).astype(jnp.bfloat16).reshape(FRESH_POSITIONS, KEY_VALUE_HEADS, query_groups * HEAD_WIDTH)
    output_projected = output_weight.reshape(KEY_VALUE_HEADS, query_groups * HEAD_WIDTH, MODEL_WIDTH).astype(jnp.float32)
    head_sums = jnp.einsum('phc,hcd->phd', attention_result.astype(jnp.float32), output_projected)
    head_sums = lax.optimization_barrier(head_sums.astype(jnp.bfloat16)).astype(jnp.float32)
    return lax.optimization_barrier(jnp.sum(head_sums, 1))

def appended_cache(single_cache, single_fresh, length):
    context = jnp.arange(CACHE_SLOT_LIMIT + FRESH_POSITIONS, dtype=jnp.int32)
    old_rows = single_cache[jnp.clip(context, 0, CACHE_SLOT_LIMIT - 1)]
    new_rows = single_fresh[jnp.clip(context - length, 0, FRESH_POSITIONS - 1)]
    later = jnp.where((context < length + FRESH_POSITIONS)[:, None], new_rows, jnp.zeros_like(new_rows))
    return jnp.where((context < length)[:, None], old_rows, later)

def reference(hidden_in, rotated_queries, fresh_key_values, cached_key_values, cached_len, expert_ids, route_gates, output_weight, norm_gain, gate_up, down_weight):
    query_req = by_request(rotated_queries)
    fresh_req = by_request(fresh_key_values)

    def one_request(packed):
        single_query, single_fresh, single_cache, length = packed
        return (request_attention(single_query, single_fresh, single_cache, length, output_weight), appended_cache(single_cache, single_fresh, length))
    attention_sum, cache_out = lax.map(one_request, (query_req, fresh_req, cached_key_values, cached_len))
    attention_dev = jnp.transpose(attention_sum.reshape(N_DP, REQ_GRP, N_TENSOR, NEW_DEV, MODEL_WIDTH), (0, 2, 1, 3, 4))
    residual = hidden_in.astype(jnp.float32) + attention_dev
    meansq = lax.optimization_barrier(jnp.mean(residual * residual, -1, keepdims=True))
    normed = (residual * lax.rsqrt(meansq + epsilon) * norm_gain).astype(jnp.bfloat16)
    blocks = N_DP * N_TENSOR
    tokens_all = blocks * TOK_DEV
    normed_flat = normed.reshape(tokens_all, MODEL_WIDTH)
    ids_block = expert_ids.reshape(blocks, TOK_DEV * TOPK)
    onehot = (ids_block[:, :, None] == jnp.arange(EXPERTS, dtype=jnp.int32)[None, None, :]).astype(jnp.int32)
    slot_rank = lax.optimization_barrier(jnp.sum(onehot * (jnp.cumsum(onehot, 1) - onehot), 2))
    slot_index = (ids_block * (blocks * CAP) + jnp.arange(blocks, dtype=jnp.int32)[:, None] * CAP + slot_rank).reshape(-1)
    token_index = jnp.arange(tokens_all * TOPK, dtype=jnp.int32) // TOPK
    slot_tokens = jnp.full((EXPERTS * blocks * CAP,), tokens_all, jnp.int32).at[slot_index].set(token_index).reshape(EXPERTS, blocks * CAP)
    gate_table = jnp.zeros((EXPERTS * blocks * CAP,), jnp.float32).at[slot_index].set(route_gates.reshape(-1).astype(jnp.float32)).reshape(EXPERTS, blocks * CAP)
    padded = jnp.concatenate([normed_flat, jnp.zeros((1, MODEL_WIDTH), jnp.bfloat16)], 0)

    def add_expert(carried, expert):
        row_index = slot_tokens[expert]
        picked = padded[row_index]
        hidden_units = jnp.dot(picked, gate_up[expert], preferred_element_type=jnp.float32)
        active = (jax.nn.silu(hidden_units[:, :FFE]) * hidden_units[:, FFE:]).astype(jnp.bfloat16)
        outputs = jnp.dot(active, down_weight[expert], preferred_element_type=jnp.float32).astype(jnp.bfloat16)
        return (carried.at[row_index].add(gate_table[expert][:, None] * outputs.astype(jnp.float32)), None)
    mixture, unused = lax.scan(add_expert, jnp.zeros((tokens_all + 1, MODEL_WIDTH), jnp.float32), jnp.arange(EXPERTS, dtype=jnp.int32))
    hidden_out = (residual.reshape(tokens_all, MODEL_WIDTH) + mixture[:tokens_all]).astype(jnp.bfloat16).reshape(hidden_in.shape)
    return (hidden_out, cache_out)
```

```python
import functools
import math

import jax
import jax.numpy as jnp
from jax import lax
from jax.experimental import pallas as pl
from jax.experimental.pallas import tpu as pltpu
from jax.sharding import PartitionSpec as P

QUERY_HEADS = 24
KEY_VALUE_HEADS = 8
HEAD_WIDTH = 64
FFE = 512

epsilon = 1e-05


def attend(q_ref, cache, fresh, length, base, out_ref):
    tokens = q_ref.shape[0]
    slots, news = cache.shape[0], fresh.shape[0]
    groups = QUERY_HEADS // KEY_VALUE_HEADS
    slot = lax.broadcasted_iota(jnp.int32, (tokens, slots), 1)
    bias_c = jnp.where(slot < length, 0.0, -1e30)[None]
    key = lax.broadcasted_iota(jnp.int32, (tokens, news), 1)
    row = lax.broadcasted_iota(jnp.int32, (tokens, news), 0)
    bias_f = jnp.where(key <= row + base, 0.0, -1e30)[None]
    low = lax.broadcasted_iota(jnp.int32, (tokens, 128), 1) < HEAD_WIDTH
    nt = (((1,), (1,)), ((), ()))
    outs = []
    for h in range(KEY_VALUE_HEADS):
        rows = []
        for g in range(groups):
            i = h * groups + g
            slab = q_ref[:, 128 * (i // 2) : 128 * (i // 2) + 128].astype(jnp.float32) * (
                1.0 / math.sqrt(HEAD_WIDTH)
            )
            if i % 2:
                slab = pltpu.roll(slab, HEAD_WIDTH, 1)
            rows.append(jnp.where(low, slab, 0.0).astype(jnp.bfloat16))
        q = jnp.concatenate(rows, 0)
        kc = cache[:, 128 * h : 128 * h + 128]
        kf = fresh[:, 128 * h : 128 * h + 128]
        sc = lax.dot_general(q, kc, nt, preferred_element_type=jnp.float32)
        sf = lax.dot_general(q, kf, nt, preferred_element_type=jnp.float32)
        sc = sc.reshape(groups, tokens, slots) + bias_c
        sf = sf.reshape(groups, tokens, news) + bias_f
        top = jnp.maximum(jnp.max(sc, -1, keepdims=True), jnp.max(sf, -1, keepdims=True))
        pc = jnp.exp(sc - top)
        pf = jnp.exp(sf - top)
        denoms = jnp.sum(pc, -1, keepdims=True) + jnp.sum(pf, -1, keepdims=True)
        pc = pc.astype(jnp.bfloat16).reshape(groups * tokens, slots)
        pf = pf.astype(jnp.bfloat16).reshape(groups * tokens, news)
        o = jnp.dot(pc, kc, preferred_element_type=jnp.float32) + jnp.dot(
            pf, kf, preferred_element_type=jnp.float32
        )
        o = o.reshape(groups, tokens, 128) / denoms
        outs += [o[g] for g in range(groups)]
        if h % 2:
            for j in range(groups):
                slab = jnp.where(low, pltpu.roll(outs[2 * j], HEAD_WIDTH, 1), outs[2 * j + 1])
                column = 128 * ((h // 2) * groups + j)
                out_ref[:, column : column + 128] = slab.astype(out_ref.dtype)
            outs = []


def attention_kernel(length_ref, q_ref, cache_ref, fresh_ref, out_ref):
    base = lax.axis_index("tensor") * q_ref.shape[0]
    attend(q_ref, cache_ref, fresh_ref, length_ref[0], base, out_ref)


def shards(
    hidden_in,
    rotated_queries,
    fresh_key_values,
    cached_key_values,
    cached_len,
    expert_ids,
    route_gates,
    output_weight,
    norm_gain,
    gate_up,
    down_weight,
):
    n = lax.axis_size("tensor")
    position = lax.axis_index("tensor")
    width = hidden_in.shape[-1]
    tokens = hidden_in.shape[2] * hidden_in.shape[3]
    kvw = fresh_key_values.shape[-1]
    cache_all = lax.all_gather(cached_key_values[0], "tensor", axis=0, tiled=True)
    fresh_all = lax.all_gather(fresh_key_values[0, 0, 0], "tensor", axis=0, tiled=True)
    weight_all = lax.all_gather(output_weight, "tensor", axis=0, tiled=True)
    ids = expert_ids.reshape(tokens, -1)
    gates = route_gates.reshape(tokens, -1)
    dense = jnp.sum(
        jnp.where(ids[:, :, None] == jnp.arange(n, dtype=jnp.int32), gates[:, :, None], 0.0), 1
    )
    dense_all = lax.all_gather(dense, "tensor", axis=0, tiled=True)
    own_gate = lax.dynamic_slice_in_dim(dense_all, position, 1, 1)
    gate_up_all = lax.all_gather(gate_up[0], "dp", axis=0, tiled=True)
    down_all = lax.all_gather(down_weight[0], "dp", axis=0, tiled=True)

    vm = pl.BlockSpec(memory_space=pltpu.VMEM)
    attended = pl.pallas_call(
        attention_kernel,
        out_shape=jax.ShapeDtypeStruct((tokens, width), jnp.bfloat16),
        in_specs=[pl.BlockSpec(memory_space=pltpu.SMEM), vm, vm, vm],
        out_specs=vm,
        compiler_params=pltpu.CompilerParams(vmem_limit_bytes=40 << 20),
        cost_estimate=pl.CostEstimate(
            flops=8 * 10**9, bytes_accessed=4 << 20, transcendentals=3 * 10**6
        ),
    )(cached_len, rotated_queries.reshape(tokens, width), cache_all, fresh_all)
    residual = hidden_in.reshape(tokens, width).astype(jnp.float32) + jnp.dot(
        attended, weight_all, preferred_element_type=jnp.float32
    )
    meansq = jnp.mean(residual * residual, -1, keepdims=True)
    normed = (residual * lax.rsqrt(meansq + epsilon) * norm_gain).astype(jnp.bfloat16)
    normed_all = lax.all_gather(normed, "tensor", axis=0, tiled=True)
    hidden_units = jnp.dot(normed_all, gate_up_all, preferred_element_type=jnp.float32)
    active = (jax.nn.silu(hidden_units[:, :FFE]) * hidden_units[:, FFE:]).astype(jnp.bfloat16)
    outputs = jnp.dot(active, down_all, preferred_element_type=jnp.float32)
    outputs = outputs.astype(jnp.bfloat16).astype(jnp.float32)
    partial = (outputs * own_gate).astype(jnp.bfloat16)
    mixture = lax.psum_scatter(partial, "tensor", scatter_dimension=0, tiled=True)
    hidden_out = (residual + mixture.astype(jnp.float32)).astype(jnp.bfloat16)

    cols = kvw // n
    length = cached_len[0]
    old = lax.dynamic_slice_in_dim(cache_all, position * cols, cols, 1)
    new = lax.dynamic_slice_in_dim(fresh_all, position * cols, cols, 1)
    total = old.shape[0] + new.shape[0]
    rows = jnp.concatenate([old, jnp.zeros_like(new)], 0)
    keep = jnp.arange(total, dtype=jnp.int32) < length
    rows = jnp.where(keep[:, None], rows, jnp.zeros_like(rows))
    cache_out = lax.dynamic_update_slice_in_dim(rows, new, length, 0)[None]
    return hidden_out.reshape(hidden_in.shape), cache_out


def solution(mesh):
    return jax.shard_map(
        shards,
        mesh=mesh,
        in_specs=(
            P("dp", "tensor", None, None, None),
            P("dp", "tensor", None, None, None),
            P("dp", "tensor", None, None, None),
            P("dp", "tensor", None),
            P("dp"),
            P("dp", "tensor", None, None, None),
            P("dp", "tensor", None, None, None),
            P("tensor", None),
            P(),
            P("tensor", "dp", None),
            P("tensor", "dp", None),
        ),
        out_specs=(P("dp", "tensor", None, None, None), P("dp", None, "tensor")),
        check_vma=False,
    )
```

```python
import functools
import math

import jax
import jax.numpy as jnp
import numpy as np
from jax import lax
from jax.experimental import pallas as pl
from jax.experimental.pallas import tpu as pltpu
from jax.sharding import PartitionSpec as P

QUERY_HEADS = 24
KEY_VALUE_HEADS = 8
HEAD_WIDTH = 64
FFE = 512

epsilon = 1e-05
CORES = 2
DEPTH = 4
FAR = 1 << 20
MESH = pl.DeviceIdType.MESH


def layer_kernel(
    n,
    n_dp,
    length_ref,
    code_ref,
    q_ref,
    hidden_ref,
    gates_ref,
    gain_ref,
    cache_hbm,
    fresh_hbm,
    weight_hbm,
    gate_up_hbm,
    down_hbm,
    out_ref,
    slab_ref,
    kv,
    wo,
    gu,
    dn,
    tok,
    part,
    from_core,
    from_x,
    from_z,
    attended,
    residual,
    local_sem,
    kv_send,
    kv_recv,
    wo_send,
    wo_recv,
    tok_send,
    tok_recv,
    gu_send,
    gu_recv,
    dn_send,
    dn_recv,
    part_send,
    core_recv,
    x_recv,
    z_recv,
):
    dp = lax.axis_index("dp")
    me = lax.axis_index("tensor")
    wide = n // (DEPTH * CORES)
    z, x, c = me // (wide * CORES), (me // CORES) % wide, me % CORES

    def index(zz, xx, cc):
        return (zz * wide + xx) * CORES + cc

    def z_of(step):
        return (z + step) % DEPTH

    def x_of(step):
        return (x + step) % wide

    other = 1 - c
    core_peer = index(z, x, other)
    z_peers = [index(z_of(s), x, c) for s in range(1, DEPTH)]
    x_peers = [index(z, x_of(s), c) for s in range(1, wide)]
    rows_peers = [(dp + s) % n_dp for s in range(1, n_dp)]

    barrier = pltpu.get_barrier_semaphore()
    for peer in z_peers + x_peers + [core_peer]:
        pl.semaphore_signal(barrier, inc=1, device_id=(dp, peer), device_id_type=MESH)
    for peer in rows_peers:
        pl.semaphore_signal(barrier, inc=1, device_id=(peer, me), device_id_type=MESH)
    cached = cache_hbm.shape[0]
    own = [
        (cache_hbm, kv.at[me, pl.ds(0, cached)]),
        (fresh_hbm, kv.at[me, pl.ds(cached, fresh_hbm.shape[0])]),
        (weight_hbm, wo.at[me]),
        (gate_up_hbm, gu.at[dp]),
        (down_hbm, dn.at[dp]),
    ]
    own = [pltpu.make_async_copy(a, b, local_sem.at[i]) for i, (a, b) in enumerate(own)]
    for copy in own:
        copy.start()
    pl.semaphore_wait(barrier, len(z_peers) + len(x_peers) + 1 + len(rows_peers))

    sent = []

    def push(source, target, send_sem, recv_sem, device):
        copy = pltpu.make_async_remote_copy(
            src_ref=source,
            dst_ref=target,
            send_sem=send_sem,
            recv_sem=recv_sem,
            device_id=device,
            device_id_type=MESH,
        )
        copy.start()
        sent.append(copy)

    def arrived(target, send_sem, recv_sem):
        pltpu.make_async_remote_copy(
            src_ref=target,
            dst_ref=target,
            send_sem=send_sem,
            recv_sem=recv_sem,
            device_id=(dp, core_peer),
            device_id_type=MESH,
        ).wait_recv()

    class Gather:
        def __init__(self, buf, send, recv):
            self.buf, self.send, self.recv, self.used = buf, send, recv, 0

        def to(self, s, peer):
            push(
                self.buf.at[s],
                self.buf.at[s],
                self.send.at[self.used],
                self.recv.at[s],
                (dp, peer),
            )
            self.used += 1

        def wait(self, s):
            arrived(self.buf.at[s], self.send.at[0], self.recv.at[s])

        def begin(self):
            for peer in z_peers + x_peers + [core_peer]:
                self.to(me, peer)

        def forward_z(self, step):
            s = index(z_of(step), x, c)
            self.wait(s)
            for peer in x_peers + [core_peer]:
                self.to(s, peer)

        def forward_x(self, hop, step):
            s = index(z_of(step), x_of(hop), c)
            self.wait(s)
            self.to(s, core_peer)

        def finish_core(self, hop):
            for step in range(DEPTH):
                self.wait(index(z_of(step), x_of(hop), other))

    keys = Gather(kv, kv_send, kv_recv)
    weights = Gather(wo, wo_send, wo_recv)
    own[0].wait()
    own[1].wait()
    keys.begin()
    for i, peer in enumerate(rows_peers):
        push(gate_up_hbm, gu.at[dp], gu_send.at[i], gu_recv.at[dp], (peer, me))
    for i, peer in enumerate(rows_peers):
        push(down_hbm, dn.at[dp], dn_send.at[i], dn_recv.at[dp], (peer, me))
    own[2].wait()
    for step in range(1, DEPTH):
        keys.forward_z(step)
    weights.begin()
    for hop in range(1, wide):
        for step in range(DEPTH):
            keys.forward_x(hop, step)
    for hop in range(wide):
        keys.finish_core(hop)

    tokens, width = q_ref.shape
    total = kv.shape[0] * kv.shape[1]
    groups = QUERY_HEADS // KEY_VALUE_HEADS
    code = jnp.broadcast_to(code_ref[...], (tokens, total))
    row = lax.broadcasted_iota(jnp.int32, (tokens, total), 0) + me * tokens
    limit = jnp.where(code < FAR, row + 1, FAR + length_ref[0])
    bias = jnp.where(code < limit, 0.0, -1e30)[None]
    low = lax.broadcasted_iota(jnp.int32, (tokens, 128), 1) < HEAD_WIDTH
    outs = []
    for h in range(KEY_VALUE_HEADS):
        rows = []
        for g in range(groups):
            i = h * groups + g
            slab = q_ref[:, 128 * (i // 2) : 128 * (i // 2) + 128].astype(jnp.float32) * (
                1.0 / math.sqrt(HEAD_WIDTH)
            )
            if i % 2:
                slab = pltpu.roll(slab, HEAD_WIDTH, 1)
            rows.append(jnp.where(low, slab, 0.0).astype(jnp.bfloat16))
        queries = jnp.concatenate(rows, 0)
        pair = kv[:, :, 128 * h : 128 * h + 128].reshape(total, 128)
        scores = lax.dot_general(
            queries, pair, (((1,), (1,)), ((), ())), preferred_element_type=jnp.float32
        )
        scores = scores.reshape(groups, tokens, total) + bias
        probs = jnp.exp(scores - jnp.max(scores, -1, keepdims=True))
        denoms = jnp.sum(probs, -1, keepdims=True)
        probs_low = probs.astype(jnp.bfloat16).reshape(groups * tokens, total)
        o = jnp.dot(probs_low, pair, preferred_element_type=jnp.float32)
        o = o.reshape(groups, tokens, 128) / denoms
        outs += [o[g] for g in range(groups)]
        if h % 2:
            for j in range(groups):
                slab = jnp.where(low, pltpu.roll(outs[2 * j], HEAD_WIDTH, 1), outs[2 * j + 1])
                column = 128 * ((h // 2) * groups + j)
                attended[:, column : column + 128] = slab.astype(attended.dtype)
            outs = []
            if h // 2 + 1 < DEPTH:
                weights.forward_z(h // 2 + 1)
    lane = pl.multiple_of(me * (kv.shape[2] // n) // 128 * 128, 128)
    slab_ref[...] = kv[:, :, pl.ds(lane, 128)]
    for hop in range(1, wide):
        for step in range(DEPTH):
            weights.forward_x(hop, step)
    for hop in range(wide):
        weights.finish_core(hop)

    projected = jnp.dot(
        attended[...], wo[...].reshape(width, width), preferred_element_type=jnp.float32
    )
    res = hidden_ref[...].astype(jnp.float32) + projected
    residual[...] = res
    meansq = jnp.mean(res * res, -1, keepdims=True)
    tok[me, :, pl.ds(0, width)] = (res * lax.rsqrt(meansq + epsilon) * gain_ref[...]).astype(
        tok.dtype
    )
    tok[me, :, pl.ds(width, 128)] = gates_ref[...]

    normed = Gather(tok, tok_send, tok_recv)
    normed.begin()
    own[3].wait()
    own[4].wait()
    for step in range(1, DEPTH):
        normed.forward_z(step)
    for peer in rows_peers:
        arrived(gu.at[peer], gu_send.at[0], gu_recv.at[peer])
        arrived(dn.at[peer], dn_send.at[0], dn_recv.at[peer])

    def experts(hop, cc):
        blocks = [index(zz, x_of(hop), cc) for zz in range(DEPTH)]
        rows = jnp.concatenate([tok[s, :, pl.ds(0, width)] for s in blocks], 0)
        marks = jnp.concatenate([tok[s, :, pl.ds(width, 128)] for s in blocks], 0)
        lanes = lax.broadcasted_iota(jnp.int32, marks.shape, 1)
        gate = jnp.sum(
            jnp.where((lanes == me) | (lanes == me + n), marks.astype(jnp.float32), 0.0),
            1,
            keepdims=True,
        )
        units = jnp.dot(
            rows, gu[...].reshape(width, 2 * FFE), preferred_element_type=jnp.float32
        )
        first = units[:, :FFE]
        active = (first / (1.0 + jnp.exp(-first)) * units[:, FFE:]).astype(jnp.bfloat16)
        result = jnp.dot(active, dn[...].reshape(FFE, width), preferred_element_type=jnp.float32)
        result = (result.astype(jnp.bfloat16).astype(jnp.float32) * gate).astype(part.dtype)
        for zz, s in enumerate(blocks):
            part[s] = result[zz * tokens : (zz + 1) * tokens]

    used = [0]

    def send_part(s, target, recv_sem, peer):
        push(part.at[s], target, part_send.at[used[0]], recv_sem, (dp, peer))
        used[0] += 1

    def send_core(hop):
        for zz in range(DEPTH):
            s = index(zz, x_of(hop), other)
            slot = zz * wide + x_of(hop)
            send_part(s, from_core.at[slot], core_recv.at[slot], core_peer)

    def add_core(hop, zz):
        s = index(zz, x_of(hop), c)
        slot = zz * wide + x_of(hop)
        arrived(from_core.at[slot], part_send.at[0], core_recv.at[slot])
        return s, part[s].astype(jnp.float32) + from_core[slot].astype(jnp.float32)

    experts(0, c)
    for hop in range(1, wide):
        for step in range(DEPTH):
            normed.forward_x(hop, step)
    normed.finish_core(0)
    experts(0, other)
    send_core(0)
    for hop in range(1, wide):
        normed.finish_core(hop)
        experts(hop, other)
        send_core(hop)
    for hop in range(1, wide):
        experts(hop, c)
        for step in range(DEPTH):
            zz = z_of((step + 1) % DEPTH)
            s, value = add_core(hop, zz)
            part[s] = value.astype(part.dtype)
            slot = (hop - 1) * DEPTH + zz
            send_part(s, from_x.at[slot], x_recv.at[slot], x_peers[hop - 1])

    final = None
    for step in range(DEPTH):
        zz = z_of((step + 1) % DEPTH)
        s, value = add_core(0, zz)
        for hop in range(1, wide):
            slot = (hop - 1) * DEPTH + zz
            arrived(from_x.at[slot], part_send.at[0], x_recv.at[slot])
            value = value + from_x[slot].astype(jnp.float32)
        if step < DEPTH - 1:
            part[s] = value.astype(part.dtype)
            send_part(s, from_z.at[step], z_recv.at[step], z_peers[step])
        else:
            final = residual[...] + value
    for step in range(DEPTH - 1):
        arrived(from_z.at[step], part_send.at[0], z_recv.at[step])
        final = final + from_z[step].astype(jnp.float32)
    out_ref[...] = final.astype(out_ref.dtype)
    for copy in sent:
        copy.wait_send()


def shards(
    hidden_in,
    rotated_queries,
    fresh_key_values,
    cached_key_values,
    cached_len,
    expert_ids,
    route_gates,
    output_weight,
    norm_gain,
    gate_up,
    down_weight,
):
    n = lax.axis_size("tensor")
    position = lax.axis_index("tensor")
    width = hidden_in.shape[-1]
    tokens = hidden_in.shape[2] * hidden_in.shape[3]
    kvw = fresh_key_values.shape[-1]
    ids = expert_ids.reshape(tokens, -1)
    gates = route_gates.reshape(tokens, -1)
    dense = jnp.sum(
        jnp.where(ids[:, :, None] == jnp.arange(n, dtype=jnp.int32), gates[:, :, None], 0.0), 1
    )
    upper = lax.reduce_precision(dense, 8, 7)
    lower = dense - upper
    marks = jnp.concatenate([upper, lower, jnp.zeros((tokens, 128 - 2 * n))], 1)
    marks = marks.astype(jnp.bfloat16)

    n_dp = lax.axis_size("dp")
    slots = cached_key_values.shape[1]
    block = slots + tokens
    code = np.concatenate(
        [
            np.arange(n)[:, None] * slots + np.arange(slots) + FAR,
            np.arange(n)[:, None] * tokens + np.arange(tokens),
        ],
        1,
    ).reshape(1, n * block)
    wide = n // (DEPTH * CORES)
    bf = jnp.bfloat16
    vm = pl.BlockSpec(memory_space=pltpu.VMEM)
    far = pl.BlockSpec(memory_space=pl.ANY)
    dma = pltpu.SemaphoreType.DMA
    hidden_out, slab = pl.pallas_call(
        functools.partial(layer_kernel, n, n_dp),
        out_shape=(
            jax.ShapeDtypeStruct((tokens, width), bf),
            jax.ShapeDtypeStruct((n, block, 128), bf),
        ),
        in_specs=[pl.BlockSpec(memory_space=pltpu.SMEM)] + [vm] * 5 + [far] * 5,
        out_specs=(vm, vm),
        scratch_shapes=[
            pltpu.VMEM((n, block, kvw), bf),
            pltpu.VMEM((n,) + output_weight.shape, bf),
            pltpu.VMEM((n_dp,) + gate_up.shape[1:], bf),
            pltpu.VMEM((n_dp,) + down_weight.shape[1:], bf),
            pltpu.VMEM((n, tokens, width + 128), bf),
            pltpu.VMEM((n, tokens, width), bf),
            pltpu.VMEM((DEPTH * wide, tokens, width), bf),
            pltpu.VMEM((DEPTH * (wide - 1), tokens, width), bf),
            pltpu.VMEM((DEPTH - 1, tokens, width), bf),
            pltpu.VMEM((tokens, width), bf),
            pltpu.VMEM((tokens, width), jnp.float32),
            dma((5,)),
            dma((n,)),
            dma((n,)),
            dma((n,)),
            dma((n,)),
            dma((n,)),
            dma((n,)),
            dma((n_dp,)),
            dma((n_dp,)),
            dma((n_dp,)),
            dma((n_dp,)),
            dma((n,)),
            dma((DEPTH * wide,)),
            dma((DEPTH * (wide - 1),)),
            dma((DEPTH - 1,)),
        ],
        compiler_params=pltpu.CompilerParams(
            collective_id=0, has_side_effects=True, vmem_limit_bytes=56 << 20
        ),
        cost_estimate=pl.CostEstimate(
            flops=10**10, bytes_accessed=8 << 20, transcendentals=4 * 10**6
        ),
    )(
        cached_len,
        jnp.asarray(code, jnp.int32),
        rotated_queries.reshape(tokens, width),
        hidden_in.reshape(tokens, width),
        marks,
        norm_gain.reshape(1, width),
        cached_key_values[0],
        fresh_key_values.reshape(tokens, kvw),
        output_weight,
        gate_up[0],
        down_weight[0],
    )

    cols = kvw // n
    length = cached_len[0]
    mine = lax.dynamic_slice_in_dim(slab, position * cols % 128, cols, 2)
    old = mine[:, :slots].reshape(n * slots, cols)
    new = mine[:, slots:].reshape(n * tokens, cols)
    total = old.shape[0] + new.shape[0]
    rows = jnp.concatenate([old, jnp.zeros_like(new)], 0)
    keep = jnp.arange(total, dtype=jnp.int32) < length
    rows = jnp.where(keep[:, None], rows, jnp.zeros_like(rows))
    cache_out = lax.dynamic_update_slice_in_dim(rows, new, length, 0)[None]
    return hidden_out.reshape(hidden_in.shape), cache_out


def solution(mesh):
    return jax.shard_map(
        shards,
        mesh=mesh,
        in_specs=(
            P("dp", "tensor", None, None, None),
            P("dp", "tensor", None, None, None),
            P("dp", "tensor", None, None, None),
            P("dp", "tensor", None),
            P("dp"),
            P("dp", "tensor", None, None, None),
            P("dp", "tensor", None, None, None),
            P("tensor", None),
            P(),
            P("tensor", "dp", None),
            P("tensor", "dp", None),
        ),
        out_specs=(P("dp", "tensor", None, None, None), P("dp", None, "tensor")),
        check_vma=False,
    )
```

```python
import functools
import math

import jax
import jax.numpy as jnp
import numpy as np
from jax import lax
from jax.experimental import pallas as pl
from jax.experimental.pallas import tpu as pltpu
from jax.sharding import PartitionSpec as P

QUERY_HEADS = 24
KEY_VALUE_HEADS = 8
HEAD_WIDTH = 64
FFE = 512

epsilon = 1e-05
CORES = 2
DEPTH = 4
FAR = 1 << 20
MESH = pl.DeviceIdType.MESH


def layer_kernel(
    n,
    n_dp,
    length_ref,
    code_ref,
    q_ref,
    hidden_ref,
    gates_ref,
    gain_ref,
    cache_ref,
    fresh_ref,
    weight_hbm,
    gate_up_hbm,
    down_hbm,
    out_ref,
    slab_ref,
    kv_out,
    q_out,
    kv,
    qs,
    wo,
    sums,
    from_plane,
    gu,
    dn,
    tok,
    part,
    from_core,
    from_x,
    from_z,
    attended,
    residual,
    local_sem,
    kv_send,
    kv_recv,
    q_send,
    q_recv,
    sums_send,
    plane_recv,
    wo_send,
    wo_recv,
    tok_send,
    tok_recv,
    gu_send,
    gu_recv,
    dn_send,
    dn_recv,
    part_send,
    core_recv,
    x_recv,
    z_recv,
):
    dp = lax.axis_index("dp")
    me = lax.axis_index("tensor")
    wide = n // (DEPTH * CORES)
    z, x, c = me // (wide * CORES), (me // CORES) % wide, me % CORES

    def index(zz, xx, cc):
        return (zz * wide + xx) * CORES + cc

    def z_of(step):
        return (z + step) % DEPTH

    def x_of(step):
        return (x + step) % wide

    other = 1 - c
    core_peer = index(z, x, other)
    z_peers = [index(z_of(s), x, c) for s in range(1, DEPTH)]
    x_peers = [index(z, x_of(s), c) for s in range(1, wide)]
    rows_peers = [(dp + s) % n_dp for s in range(1, n_dp)]

    barrier = pltpu.get_barrier_semaphore()
    for peer in z_peers + x_peers + [core_peer]:
        pl.semaphore_signal(barrier, inc=1, device_id=(dp, peer), device_id_type=MESH)
    for peer in rows_peers:
        pl.semaphore_signal(barrier, inc=1, device_id=(peer, me), device_id_type=MESH)
    spot = x * CORES + c
    own = [
        (weight_hbm, wo.at[spot]),
        (gate_up_hbm, gu.at[dp]),
        (down_hbm, dn.at[dp]),
    ]
    own = [pltpu.make_async_copy(a, b, local_sem.at[i]) for i, (a, b) in enumerate(own)]
    for copy in own:
        copy.start()
    cached, span = cache_ref.shape[0], kv.shape[2]
    reach = qs.shape[2]
    for zz in range(DEPTH):
        kv_out[zz, :cached] = cache_ref[:, zz * span : (zz + 1) * span]
        kv_out[zz, cached:] = fresh_ref[:, zz * span : (zz + 1) * span]
        q_out[zz] = q_ref[:, zz * reach : (zz + 1) * reach]
    kv[me] = kv_out[z]
    qs[z] = q_out[z]
    pl.semaphore_wait(barrier, len(z_peers) + len(x_peers) + 1 + len(rows_peers))

    sent = []

    def push(source, target, send_sem, recv_sem, device):
        copy = pltpu.make_async_remote_copy(
            src_ref=source,
            dst_ref=target,
            send_sem=send_sem,
            recv_sem=recv_sem,
            device_id=device,
            device_id_type=MESH,
        )
        copy.start()
        sent.append(copy)

    def arrived(target, send_sem, recv_sem):
        pltpu.make_async_remote_copy(
            src_ref=target,
            dst_ref=target,
            send_sem=send_sem,
            recv_sem=recv_sem,
            device_id=(dp, core_peer),
            device_id_type=MESH,
        ).wait_recv()

    class Gather:
        def __init__(self, buf, send, recv):
            self.buf, self.send, self.recv, self.used = buf, send, recv, 0

        def to(self, s, peer):
            push(
                self.buf.at[s],
                self.buf.at[s],
                self.send.at[self.used],
                self.recv.at[s],
                (dp, peer),
            )
            self.used += 1

        def wait(self, s):
            arrived(self.buf.at[s], self.send.at[0], self.recv.at[s])

        def begin(self):
            for peer in z_peers + x_peers + [core_peer]:
                self.to(me, peer)

        def forward_z(self, step):
            s = index(z_of(step), x, c)
            self.wait(s)
            for peer in x_peers + [core_peer]:
                self.to(s, peer)

        def forward_x(self, hop, step):
            s = index(z_of(step), x_of(hop), c)
            self.wait(s)
            self.to(s, core_peer)

        def finish_core(self, hop):
            for step in range(DEPTH):
                self.wait(index(z_of(step), x_of(hop), other))

    keys = Gather(kv, kv_send, kv_recv)
    for step, peer in enumerate(z_peers, 1):
        push(
            kv_out.at[z_of(step)],
            kv.at[me],
            kv_send.at[keys.used],
            kv_recv.at[me],
            (dp, peer),
        )
        keys.used += 1
    for peer in x_peers + [core_peer]:
        keys.to(me, peer)
    for step, peer in enumerate(z_peers, 1):
        push(
            q_out.at[z_of(step)], qs.at[z], q_send.at[step - 1], q_recv.at[z], (dp, peer)
        )
    for i, peer in enumerate(rows_peers):
        push(gate_up_hbm, gu.at[dp], gu_send.at[i], gu_recv.at[dp], (peer, me))
    for i, peer in enumerate(rows_peers):
        push(down_hbm, dn.at[dp], dn_send.at[i], dn_recv.at[dp], (peer, me))
    for step in range(1, DEPTH):
        keys.forward_z(step)
    own[0].wait()
    for i, peer in enumerate(x_peers + [core_peer]):
        push(wo.at[spot], wo.at[spot], wo_send.at[i], wo_recv.at[spot], (dp, peer))
    for hop in range(1, wide):
        for step in range(DEPTH):
            keys.forward_x(hop, step)
    for hop in range(1, wide):
        there = x_of(hop) * CORES + c
        arrived(wo.at[there], wo_send.at[0], wo_recv.at[there])
        push(
            wo.at[there],
            wo.at[there],
            wo_send.at[wide - 1 + hop],
            wo_recv.at[there],
            (dp, core_peer),
        )
    for hop in range(wide):
        keys.finish_core(hop)

    tokens, width = q_ref.shape
    total = kv.shape[0] * kv.shape[1]
    groups = QUERY_HEADS // KEY_VALUE_HEADS
    code = jnp.broadcast_to(code_ref[...], (tokens, total))
    low = lax.broadcasted_iota(jnp.int32, (tokens, 128), 1) < HEAD_WIDTH

    def attend(zz):
        base = index(zz, x, c) * tokens
        row = lax.broadcasted_iota(jnp.int32, (tokens, total), 0) + base
        limit = jnp.where(code < FAR, row + 1, FAR + length_ref[0])
        bias = jnp.where(code < limit, 0.0, -1e30)[None]
        outs = []
        for h in range(KEY_VALUE_HEADS // DEPTH):
            rows = []
            for g in range(groups):
                i = h * groups + g
                slab = qs[zz, :, pl.ds(128 * (i // 2), 128)].astype(jnp.float32) * (
                    1.0 / math.sqrt(HEAD_WIDTH)
                )
                if i % 2:
                    slab = pltpu.roll(slab, HEAD_WIDTH, 1)
                rows.append(jnp.where(low, slab, 0.0).astype(jnp.bfloat16))
            queries = jnp.concatenate(rows, 0)
            pair = kv[:, :, 128 * h : 128 * h + 128].reshape(total, 128)
            scores = lax.dot_general(
                queries, pair, (((1,), (1,)), ((), ())), preferred_element_type=jnp.float32
            )
            scores = scores.reshape(groups, tokens, total) + bias
            probs = jnp.exp(scores - jnp.max(scores, -1, keepdims=True))
            denoms = jnp.sum(probs, -1, keepdims=True)
            probs_low = probs.astype(jnp.bfloat16).reshape(groups * tokens, total)
            o = jnp.dot(probs_low, pair, preferred_element_type=jnp.float32)
            o = o.reshape(groups, tokens, 128) / denoms
            outs += [o[g] for g in range(groups)]
        for j in range(len(outs) // 2):
            slab = jnp.where(low, pltpu.roll(outs[2 * j], HEAD_WIDTH, 1), outs[2 * j + 1])
            attended[:, 128 * j : 128 * j + 128] = slab.astype(attended.dtype)

    def projected():
        return jnp.dot(
            attended[...], wo[...].reshape(reach, width), preferred_element_type=jnp.float32
        )

    for step in range(1, DEPTH):
        zz = z_of(step)
        arrived(qs.at[zz], q_send.at[0], q_recv.at[zz])
        attend(zz)
        if step == 1:
            for hop in range(wide):
                there = x_of(hop) * CORES + other
                arrived(wo.at[there], wo_send.at[0], wo_recv.at[there])
        sums[step - 1] = projected().astype(sums.dtype)
        push(
            sums.at[step - 1],
            from_plane.at[step - 1],
            sums_send.at[step - 1],
            plane_recv.at[step - 1],
            (dp, z_peers[step - 1]),
        )
    attend(z)
    lane = pl.multiple_of(me * (span * DEPTH // n) // 128 * 128 - z * span, 128)
    slab_ref[...] = kv[:, :, pl.ds(lane, 128)]

    res = hidden_ref[...].astype(jnp.float32) + projected()
    for step in range(DEPTH - 1):
        arrived(from_plane.at[step], sums_send.at[0], plane_recv.at[step])
        res = res + from_plane[step].astype(jnp.float32)
    residual[...] = res
    meansq = jnp.mean(res * res, -1, keepdims=True)
    tok[me, :, pl.ds(0, width)] = (res * lax.rsqrt(meansq + epsilon) * gain_ref[...]).astype(
        tok.dtype
    )
    tok[me, :, pl.ds(width, 128)] = gates_ref[...]

    normed = Gather(tok, tok_send, tok_recv)
    normed.begin()
    own[1].wait()
    own[2].wait()
    for step in range(1, DEPTH):
        normed.forward_z(step)
    for peer in rows_peers:
        arrived(gu.at[peer], gu_send.at[0], gu_recv.at[peer])
        arrived(dn.at[peer], dn_send.at[0], dn_recv.at[peer])

    def experts(hop, cc):
        blocks = [index(zz, x_of(hop), cc) for zz in range(DEPTH)]
        rows = jnp.concatenate([tok[s, :, pl.ds(0, width)] for s in blocks], 0)
        marks = jnp.concatenate([tok[s, :, pl.ds(width, 128)] for s in blocks], 0)
        lanes = lax.broadcasted_iota(jnp.int32, marks.shape, 1)
        gate = jnp.sum(
            jnp.where((lanes == me) | (lanes == me + n), marks.astype(jnp.float32), 0.0),
            1,
            keepdims=True,
        )
        units = jnp.dot(
            rows, gu[...].reshape(width, 2 * FFE), preferred_element_type=jnp.float32
        )
        first = units[:, :FFE]
        active = (first / (1.0 + jnp.exp(-first)) * units[:, FFE:]).astype(jnp.bfloat16)
        result = jnp.dot(active, dn[...].reshape(FFE, width), preferred_element_type=jnp.float32)
        result = (result.astype(jnp.bfloat16).astype(jnp.float32) * gate).astype(part.dtype)
        for zz, s in enumerate(blocks):
            part[s] = result[zz * tokens : (zz + 1) * tokens]

    used = [0]

    def send_part(s, target, recv_sem, peer):
        push(part.at[s], target, part_send.at[used[0]], recv_sem, (dp, peer))
        used[0] += 1

    def send_core(hop):
        for zz in range(DEPTH):
            s = index(zz, x_of(hop), other)
            slot = zz * wide + x_of(hop)
            send_part(s, from_core.at[slot], core_recv.at[slot], core_peer)

    def add_core(hop, zz):
        s = index(zz, x_of(hop), c)
        slot = zz * wide + x_of(hop)
        arrived(from_core.at[slot], part_send.at[0], core_recv.at[slot])
        return s, part[s].astype(jnp.float32) + from_core[slot].astype(jnp.float32)

    experts(0, c)
    for hop in range(1, wide):
        for step in range(DEPTH):
            normed.forward_x(hop, step)
    normed.finish_core(0)
    experts(0, other)
    send_core(0)
    for hop in range(1, wide):
        normed.finish_core(hop)
        experts(hop, other)
        send_core(hop)
    for hop in range(1, wide):
        experts(hop, c)
        for step in range(DEPTH):
            zz = z_of((step + 1) % DEPTH)
            s, value = add_core(hop, zz)
            part[s] = value.astype(part.dtype)
            slot = (hop - 1) * DEPTH + zz
            send_part(s, from_x.at[slot], x_recv.at[slot], x_peers[hop - 1])

    final = None
    for step in range(DEPTH):
        zz = z_of((step + 1) % DEPTH)
        s, value = add_core(0, zz)
        for hop in range(1, wide):
            slot = (hop - 1) * DEPTH + zz
            arrived(from_x.at[slot], part_send.at[0], x_recv.at[slot])
            value = value + from_x[slot].astype(jnp.float32)
        if step < DEPTH - 1:
            part[s] = value.astype(part.dtype)
            send_part(s, from_z.at[step], z_recv.at[step], z_peers[step])
        else:
            final = residual[...] + value
    for step in range(DEPTH - 1):
        arrived(from_z.at[step], part_send.at[0], z_recv.at[step])
        final = final + from_z[step].astype(jnp.float32)
    out_ref[...] = final.astype(out_ref.dtype)
    for copy in sent:
        copy.wait_send()


def shards(
    hidden_in,
    rotated_queries,
    fresh_key_values,
    cached_key_values,
    cached_len,
    expert_ids,
    route_gates,
    output_weight,
    norm_gain,
    gate_up,
    down_weight,
):
    n = lax.axis_size("tensor")
    position = lax.axis_index("tensor")
    width = hidden_in.shape[-1]
    tokens = hidden_in.shape[2] * hidden_in.shape[3]
    kvw = fresh_key_values.shape[-1]
    ids = expert_ids.reshape(tokens, -1)
    gates = route_gates.reshape(tokens, -1)
    dense = jnp.sum(
        jnp.where(ids[:, :, None] == jnp.arange(n, dtype=jnp.int32), gates[:, :, None], 0.0), 1
    )
    upper = lax.reduce_precision(dense, 8, 7)
    lower = dense - upper
    marks = jnp.concatenate([upper, lower, jnp.zeros((tokens, 128 - 2 * n))], 1)
    marks = marks.astype(jnp.bfloat16)

    n_dp = lax.axis_size("dp")
    slots = cached_key_values.shape[1]
    block = slots + tokens
    code = np.concatenate(
        [
            np.arange(n)[:, None] * slots + np.arange(slots) + FAR,
            np.arange(n)[:, None] * tokens + np.arange(tokens),
        ],
        1,
    ).reshape(1, n * block)
    wide = n // (DEPTH * CORES)
    bf = jnp.bfloat16
    vm = pl.BlockSpec(memory_space=pltpu.VMEM)
    far = pl.BlockSpec(memory_space=pl.ANY)
    dma = pltpu.SemaphoreType.DMA
    hidden_out, slab = pl.pallas_call(
        functools.partial(layer_kernel, n, n_dp),
        out_shape=(
            jax.ShapeDtypeStruct((tokens, width), bf),
            jax.ShapeDtypeStruct((n, block, 128), bf),
        ),
        in_specs=[pl.BlockSpec(memory_space=pltpu.SMEM)] + [vm] * 7 + [far] * 3,
        out_specs=(vm, vm),
        scratch_shapes=[
            pltpu.VMEM((DEPTH, block, kvw // DEPTH), bf),
            pltpu.VMEM((DEPTH, tokens, width // DEPTH), bf),
            pltpu.VMEM((n, block, kvw // DEPTH), bf),
            pltpu.VMEM((DEPTH, tokens, width // DEPTH), bf),
            pltpu.VMEM((n // DEPTH,) + output_weight.shape, bf),
            pltpu.VMEM((DEPTH - 1, tokens, width), bf),
            pltpu.VMEM((DEPTH - 1, tokens, width), bf),
            pltpu.VMEM((n_dp,) + gate_up.shape[1:], bf),
            pltpu.VMEM((n_dp,) + down_weight.shape[1:], bf),
            pltpu.VMEM((n, tokens, width + 128), bf),
            pltpu.VMEM((n, tokens, width), bf),
            pltpu.VMEM((DEPTH * wide, tokens, width), bf),
            pltpu.VMEM((DEPTH * (wide - 1), tokens, width), bf),
            pltpu.VMEM((DEPTH - 1, tokens, width), bf),
            pltpu.VMEM((tokens, width // DEPTH), bf),
            pltpu.VMEM((tokens, width), jnp.float32),
            dma((3,)),
            dma((n,)),
            dma((n,)),
            dma((DEPTH - 1,)),
            dma((DEPTH,)),
            dma((DEPTH - 1,)),
            dma((DEPTH - 1,)),
            dma((n,)),
            dma((n,)),
            dma((n,)),
            dma((n,)),
            dma((n_dp,)),
            dma((n_dp,)),
            dma((n_dp,)),
            dma((n_dp,)),
            dma((n,)),
            dma((DEPTH * wide,)),
            dma((DEPTH * (wide - 1),)),
            dma((DEPTH - 1,)),
        ],
        compiler_params=pltpu.CompilerParams(
            collective_id=0, has_side_effects=True, vmem_limit_bytes=56 << 20
        ),
        cost_estimate=pl.CostEstimate(
            flops=10**10, bytes_accessed=8 << 20, transcendentals=4 * 10**6
        ),
    )(
        cached_len,
        jnp.asarray(code, jnp.int32),
        rotated_queries.reshape(tokens, width),
        hidden_in.reshape(tokens, width),
        marks,
        norm_gain.reshape(1, width),
        cached_key_values[0],
        fresh_key_values.reshape(tokens, kvw),
        output_weight,
        gate_up[0],
        down_weight[0],
    )

    cols = kvw // n
    length = cached_len[0]
    mine = lax.dynamic_slice_in_dim(slab, position * cols % 128, cols, 2)
    old = mine[:, :slots].reshape(n * slots, cols)
    new = mine[:, slots:].reshape(n * tokens, cols)
    total = old.shape[0] + new.shape[0]
    rows = jnp.concatenate([old, jnp.zeros_like(new)], 0)
    keep = jnp.arange(total, dtype=jnp.int32) < length
    rows = jnp.where(keep[:, None], rows, jnp.zeros_like(rows))
    cache_out = lax.dynamic_update_slice_in_dim(rows, new, length, 0)[None]
    return hidden_out.reshape(hidden_in.shape), cache_out


def solution(mesh):
    return jax.shard_map(
        shards,
        mesh=mesh,
        in_specs=(
            P("dp", "tensor", None, None, None),
            P("dp", "tensor", None, None, None),
            P("dp", "tensor", None, None, None),
            P("dp", "tensor", None),
            P("dp"),
            P("dp", "tensor", None, None, None),
            P("dp", "tensor", None, None, None),
            P("tensor", None),
            P(),
            P("tensor", "dp", None),
            P("tensor", "dp", None),
        ),
        out_specs=(P("dp", "tensor", None, None, None), P("dp", None, "tensor")),
        check_vma=False,
    )
```
